32 devices in a mesh: ctx: 8 (over z, core), tp: 4 (over y, x).
Axes of the slice: x: 2, y: 2, z: 4, core: 2. Of those that a mesh axis runs over, the one named last changes fastest.
Arguments:
- queries: bfloat16 [4096, 2048], P('ctx', 'tp'), may hold values from -6 to 6
- key_rows: bfloat16 [4096, 2048], P('ctx', 'tp'), may hold values from -6 to 6
- value_rows: bfloat16 [4096, 2048], P('ctx', 'tp'), may hold values from -30 to 30
- selection: int32 [8, 3], replicated, may hold values from 0 to 7, as said below
- out_weight: bfloat16 [2048, 7168], P('tp'), may hold values from -0.1875 to 0.1875
Outputs:
- mixed: bfloat16 [4096, 7168], P('ctx', 'tp')
The draws below stay inside these ranges and needn't reach their ends.
Inputs may be any that keep to these rules, and one draw needn't show every extreme that they name: Row q of selection lists q first, then 3 - 1 distinct blocks below q; where fewer than that lie below q, the remaining entries are q.
All inputs are finite; a program needn't handle non-finite values.
Results may differ from the reference program's by a relative error of at most 0.013.
Values may be sent and summed in bfloat16 or wider, within the bound.
A program may use at most 192 MiB of HBM per device.

```python
import jax
import jax.numpy as jnp
from jax import lax

D = 7168
HD = 128
BLOCK = 512
TOPK = 3
HEADS = 16
NB = 8
TOKENS = 4096


def paired_rows(key):
    base = jax.random.fold_in(key, 7)
    key_query, key_keys = jax.random.split(base, 2)
    shape = (TOKENS, HEADS * HD)
    query_vals = jnp.clip(1.3 * jax.random.normal(key_query, shape, jnp.float32), -6.0, 6.0)
    key_vals = jnp.clip(1.3 * jax.random.normal(key_keys, shape, jnp.float32), -6.0, 6.0)
    return (query_vals, key_vals)


def draw_queries(key, part):
    return paired_rows(key)[0].astype(jnp.bfloat16)


def draw_key_rows(key, part):
    return paired_rows(key)[1].astype(jnp.bfloat16)


def draw_selection(key, part):
    block_rows = jnp.arange(NB, dtype=jnp.int32)[:, None]
    block_cols = jnp.arange(NB, dtype=jnp.int32)[None, :]
    random_part = jax.random.randint(jax.random.fold_in(key, 3), (NB, NB), 0, 1 << 16)
    valid_score = random_part * NB + block_cols + NB
    other_score = NB - 1 - (block_cols - block_rows)
    scores = jnp.where(block_cols < block_rows, valid_score, other_score).astype(jnp.int32)
    _, picked = jax.lax.top_k(scores, TOPK - 1)
    picked = jnp.where(picked <= block_rows, picked, block_rows).astype(jnp.int32)
    return jnp.concatenate([block_rows, picked], axis=1).astype(jnp.int32)


def with_spikes(drawn, stream_key, source, target, blocks, factor):
    def block_of(dim):
        return (jnp.arange(drawn.shape[dim]) // (drawn.shape[dim] // blocks)).reshape((-1,) + (1,) * (drawn.ndim - 1 - dim))

    first = jax.random.permutation(stream_key, blocks)[block_of(target)]
    other_side = (block_of(target) + blocks // 2) % blocks
    return jnp.where((block_of(source) == first) | (block_of(source) == other_side), factor * drawn, drawn)


def block_scale(rng, shape, cuts, least, high):
    factor_of, own = 1.0, jax.random.fold_in(rng, 6)
    for position, blocks in cuts:
        draws = jnp.exp(jax.random.uniform(jax.random.fold_in(own, position), (blocks,), jnp.float32, least / len(cuts), high / len(cuts)))
        factor_of = factor_of * jnp.repeat(draws, shape[position] // blocks).reshape([-1 if axis == position else 1 for axis in range(len(shape))])
    return factor_of


def gaussian(own_key, shape, spread, reach, pieces=(), held_as=jnp.bfloat16):
    array = spread * jax.random.normal(own_key, shape, jnp.float32)
    if pieces:
        array = array * block_scale(own_key, shape, pieces, -0.22, 0.18)
    return jnp.clip(array, -reach, reach).astype(held_as)


def bell_draw_with(stream_key, dims, width, limit, cuts, heavy, kind=jnp.bfloat16):
    array = width * jax.random.normal(stream_key, dims, jnp.float32)
    if cuts:
        array = array * block_scale(stream_key, dims, cuts, -0.22, 0.18)
    return jnp.clip(with_spikes(array, jax.random.fold_in(stream_key, 3), *heavy), -limit, limit).astype(kind)


def setup_inputs(seed: int = 0) -> dict:
    streams_of = jax.random.split(jax.random.key(seed), 6)
    return {
        "queries": draw_queries(jax.random.fold_in(streams_of[5], 71), 0),
        "key_rows": draw_key_rows(jax.random.fold_in(streams_of[5], 71), 0),
        "value_rows": gaussian(streams_of[2], (TOKENS, HEADS * HD), 5.0, 30.0, ((0, 8), (1, 4))),
        "selection": draw_selection(jax.random.fold_in(streams_of[5], 71), 0),
        "out_weight": bell_draw_with(streams_of[4], (HEADS * HD, D), (HEADS * HD) ** -0.5, 0.1875, ((0, 4),), (0, 1, 4, 2.0)),
    }


def reference(queries, key_rows, value_rows, selection, out_weight):
    query_blocks = queries.reshape(NB, BLOCK, HEADS, HD)
    key_blocks = key_rows.reshape(NB, BLOCK, HEADS, HD)
    value_blocks = value_rows.reshape(NB, BLOCK, HEADS, HD)
    scaling = 1.0 / jnp.sqrt(jnp.float32(HD))

    def block_out(block_index):
        listed = selection[block_index].astype(jnp.int32)
        repeated = jnp.concatenate([jnp.zeros((1,), bool), listed[1:] == listed[0]])
        picked_keys = jnp.take(key_blocks, listed, axis=0).reshape(TOPK * BLOCK, HEADS, HD)
        picked_values = jnp.take(value_blocks, listed, axis=0).reshape(TOPK * BLOCK, HEADS, HD)
        query_pos = block_index * BLOCK + jnp.arange(BLOCK, dtype=jnp.int32)
        key_pos = (listed[:, None] * BLOCK + jnp.arange(BLOCK, dtype=jnp.int32)[None, :]).reshape(-1)
        usable = jnp.repeat(jnp.logical_not(repeated), BLOCK)
        allowed = (key_pos[None, :] <= query_pos[:, None]) & usable[None, :]
        scores = jnp.einsum('thd,shd->hts', query_blocks[block_index].astype(jnp.float32), picked_keys.astype(jnp.float32)) * scaling
        row_max = lax.optimization_barrier(jnp.max(jnp.where(allowed[None], scores, -jnp.inf), axis=-1))
        expo = jnp.where(allowed[None], jnp.exp(scores - row_max[..., None]), 0.0)
        row_sum = lax.optimization_barrier(jnp.sum(expo, axis=-1))
        weights = lax.optimization_barrier(expo.astype(jnp.bfloat16))
        numer = jnp.einsum('hts,shd->thd', weights.astype(jnp.float32), picked_values.astype(jnp.float32))
        result = numer / jnp.transpose(row_sum)[..., None]
        return result.astype(jnp.bfloat16).reshape(BLOCK, HEADS * HD)
    attended = lax.map(block_out, jnp.arange(NB, dtype=jnp.int32)).reshape(TOKENS, HEADS * HD)
    return jnp.dot(attended, out_weight, preferred_element_type=jnp.float32).astype(jnp.bfloat16)
```

```python
import functools

import jax
import jax.numpy as jnp
from jax import lax
from jax.experimental import pallas as pl
from jax.experimental.pallas import tpu as pltpu
from jax.sharding import PartitionSpec as P

HD = 128
BLOCK = 512
NEG = -1e30
MESH = pl.DeviceIdType.MESH
SCALE2 = 1.4426950408889634 / HD**0.5


def kernel(
    n_ctx, n_tp, heads,
    q_ref, k_ref, v_ref, sel_ref, w_ref, out_ref,
    *scratch,
):
    kv = scratch[:heads]
    (wbuf, att, acc, up_send, up_recv, sib_send, sib_recv, w_send, w_recv,
     ws_send, ws_recv, att_send, att_recv) = scratch[heads:]
    chips = n_ctx // 2
    group = heads // 2
    gk = group * HD
    cols = out_ref.shape[1]
    ctx = lax.axis_index("ctx")
    tp = lax.axis_index("tp")
    z, c = ctx // 2, ctx % 2
    sib = z * 2 + 1 - c
    above, below = ctx + 2, ctx - 2
    not_last = z < chips - 1

    barrier = pltpu.get_barrier_semaphore()

    def greet(**where):
        pl.semaphore_signal(barrier, inc=1, device_id=where, device_id_type=MESH)

    greet(ctx=sib)
    for d in range(1, n_tp):
        greet(tp=(tp + d) % n_tp)

    @pl.when(not_last)
    def _():
        greet(ctx=above)

    @pl.when(z > 0)
    def _():
        greet(ctx=below)

    ends = (z == 0).astype(jnp.int32) + (z == chips - 1).astype(jnp.int32)
    pl.semaphore_wait(barrier, n_tp + 2 - ends)

    def remote(src, dst, send, recv, **where):
        return pltpu.make_async_remote_copy(
            src_ref=src, dst_ref=dst, send_sem=send, recv_sem=recv,
            device_id=where, device_id_type=MESH,
        )

    def up(h, zz):
        slot = kv[h].at[zz * 2 + c]
        return remote(slot, slot, up_send.at[h, zz], up_recv.at[h, zz], ctx=above)

    def from_below(h, zz):
        slot = kv[h].at[zz * 2 + c]
        return remote(slot, slot, up_send.at[h, zz], up_recv.at[h, zz], ctx=below)

    def side(h, zz):
        slot = kv[h].at[zz * 2 + c]
        return remote(slot, slot, sib_send.at[h, zz], sib_recv.at[h, zz], ctx=sib)

    def from_side(h, zz):
        slot = kv[h].at[zz * 2 + 1 - c]
        return remote(slot, slot, sib_send.at[h, zz], sib_recv.at[h, zz], ctx=sib)

    def send_on(h, zz):
        @pl.when(not_last)
        def _():
            up(h, zz).start()

        side(h, zz).start()

    def w_rows(half, p):
        return wbuf.at[half, pl.ds(pl.multiple_of(p * gk, gk), gk)]

    def w_out(p):
        src = w_ref.at[pl.ds(pl.multiple_of(c * gk, gk), gk), pl.ds(pl.multiple_of(p * cols, 128), cols)]
        return remote(src, w_rows(c, tp), w_send.at[p], w_recv.at[tp], tp=p)

    def w_in(p):
        return remote(w_rows(c, p), w_rows(c, p), w_send.at[p], w_recv.at[p], tp=p)

    def w_side(p):
        return remote(w_rows(c, p), w_rows(c, p), ws_send.at[p], ws_recv.at[p], ctx=sib)

    def w_from_side(p):
        return remote(w_rows(1 - c, p), w_rows(1 - c, p), ws_send.at[p], ws_recv.at[p], ctx=sib)

    def w_own(half):
        src = w_ref.at[half * gk:(half + 1) * gk, pl.ds(pl.multiple_of(tp * cols, 128), cols)]
        sem = w_send if half == 0 else ws_send
        return pltpu.make_async_copy(src, w_rows(half, tp), sem.at[tp])

    def att_slot(h, p):
        start = p * gk + (h % group) * HD
        return att.at[h // group, :, pl.ds(pl.multiple_of(start, HD), HD)]

    def att_out(h, p):
        return remote(att_slot(h, tp), att_slot(h, tp), att_send.at[h, p], att_recv.at[h, tp], tp=p)

    def att_in(h, p):
        return remote(att_slot(h, p), att_slot(h, p), att_send.at[h, p], att_recv.at[h, p], tp=p)

    peers = [(tp + d) % n_tp for d in range(1, n_tp)]

    def own_block(h):
        kv[h][ctx, 0] = k_ref[:, h * HD:(h + 1) * HD]
        kv[h][ctx, 1] = v_ref[:, h * HD:(h + 1) * HD]
        send_on(h, z)

    own_block(0)
    for p in peers:
        w_out(p).start()
    w_own(0).start()
    w_own(1).start()

    first, second = sel_ref[ctx, 1], sel_ref[ctx, 2]
    bias1 = jnp.where(first == ctx, jnp.float32(NEG), jnp.float32(0))
    bias2 = jnp.where(second == ctx, jnp.float32(NEG), jnp.float32(0))
    contract = (((1,), (1,)), ((), ()))

    def attend(h):
        rows = 256
        k1, v1 = kv[h][first, 0], kv[h][first, 1]
        k2, v2 = kv[h][second, 0], kv[h][second, 1]
        for r in range(BLOCK // rows):
            depth = (r + 1) * rows
            q = q_ref[r * rows:(r + 1) * rows, h * HD:(h + 1) * HD]
            k0 = k_ref[:depth, h * HD:(h + 1) * HD]
            v0 = v_ref[:depth, h * HD:(h + 1) * HD]

            def score(k):
                return lax.dot_general(q, k, contract, preferred_element_type=jnp.float32)

            s0, s1, s2 = score(k0), score(k1) + bias1, score(k2) + bias2
            rid = lax.broadcasted_iota(jnp.int32, s0.shape, 0) + r * rows
            cid = lax.broadcasted_iota(jnp.int32, s0.shape, 1)
            s0 = jnp.where(cid <= rid, s0, NEG)
            top = jnp.maximum(
                jnp.max(s0, axis=1, keepdims=True),
                jnp.maximum(jnp.max(s1, axis=1, keepdims=True), jnp.max(s2, axis=1, keepdims=True)),
            )
            e0, e1, e2 = (jnp.exp2((s - top) * SCALE2) for s in (s0, s1, s2))
            total = (
                jnp.sum(e0, axis=1, keepdims=True)
                + jnp.sum(e1, axis=1, keepdims=True)
                + jnp.sum(e2, axis=1, keepdims=True)
            )
            numer = sum(
                jnp.dot(e.astype(jnp.bfloat16), v, preferred_element_type=jnp.float32)
                for e, v in ((e0, v0), (e1, v1), (e2, v2))
            )
            start = pl.multiple_of(tp * gk + (h % group) * HD, HD)
            att[h // group, r * rows:(r + 1) * rows, pl.ds(start, HD)] = (numer / total).astype(jnp.bfloat16)
        for p in peers:
            att_out(h, p).start()

    tile = 256 if cols % 256 == 0 else 128

    def project(g):
        for h in range(g * group, (g + 1) * group):
            for p in peers:
                att_in(h, p).wait_recv()

        @pl.loop(0, cols // tile)
        def _(n):
            at = pl.ds(pl.multiple_of(n * tile, tile), tile)
            part = jnp.dot(att[g], wbuf[g, :, at], preferred_element_type=jnp.float32)
            if g == 0:
                acc[:, at] = part
            else:
                out_ref[:, at] = (acc[:, at] + part).astype(out_ref.dtype)

    for h in range(heads):
        if h + 1 < heads:
            own_block(h + 1)
        if h == heads - 1:
            for p in peers:
                w_in(p).wait_recv()
                w_side(p).start()

        @pl.loop(0, z)
        def _(s):
            zz = z - 1 - s
            from_below(h, zz).wait_recv()
            send_on(h, zz)

        if h == heads - 1:
            w_own(0).wait()
            w_own(1).wait()
            for p in peers:
                w_from_side(p).wait_recv()
            project(0)

        @pl.loop(0, z + 1)
        def _(zz):
            from_side(h, zz).wait_recv()

        attend(h)
    project(1)

    for h in range(heads):
        @pl.loop(0, z + 1)
        def _(zz):
            side(h, zz).wait_send()

            @pl.when(not_last)
            def _():
                up(h, zz).wait_send()

        for p in peers:
            att_out(h, p).wait_send()
    for p in peers:
        w_out(p).wait_send()
        w_side(p).wait_send()


def per_device(n_ctx, n_tp, queries, key_rows, value_rows, selection, out_weight):
    rows, width = queries.shape
    heads = width // HD
    cols = out_weight.shape[1] // n_tp
    gk = heads // 2 * HD
    chips = n_ctx // 2
    vmem = pl.BlockSpec(memory_space=pltpu.VMEM)
    dma = pltpu.SemaphoreType.DMA
    return pl.pallas_call(
        functools.partial(kernel, n_ctx, n_tp, heads),
        out_shape=jax.ShapeDtypeStruct((rows, cols), jnp.bfloat16),
        in_specs=[
            vmem, vmem, vmem,
            pl.BlockSpec(memory_space=pltpu.SMEM),
            pl.BlockSpec(memory_space=pl.ANY),
        ],
        out_specs=vmem,
        scratch_shapes=[pltpu.VMEM((n_ctx, 2, BLOCK, HD), jnp.bfloat16) for _ in range(heads)] + [
            pltpu.VMEM((2, n_tp * gk, cols), jnp.bfloat16),
            pltpu.VMEM((2, rows, n_tp * gk), jnp.bfloat16),
            pltpu.VMEM((rows, cols), jnp.float32),
            dma((heads, chips)), dma((heads, chips)),
            dma((heads, chips)), dma((heads, chips)),
            dma((n_tp,)), dma((n_tp,)), dma((n_tp,)), dma((n_tp,)),
            dma((heads, n_tp)), dma((heads, n_tp)),
        ],
        compiler_params=pltpu.CompilerParams(
            collective_id=0, has_side_effects=True, vmem_limit_bytes=52 * 2**20
        ),
        cost_estimate=pl.CostEstimate(
            flops=2 * rows * cols * n_tp * width + 12 * rows * BLOCK * width,
            bytes_accessed=2 * (out_weight.size + 4 * rows * width),
            transcendentals=3 * rows * BLOCK * heads,
        ),
    )(queries, key_rows, value_rows, selection, out_weight)


def solution(mesh):
    placed = (P("ctx", "tp"), P("ctx", "tp"), P("ctx", "tp"), P(), P("tp", None))
    body = functools.partial(per_device, mesh.shape["ctx"], mesh.shape["tp"])
    return jax.shard_map(
        body, mesh=mesh, in_specs=placed, out_specs=P("ctx", "tp"), check_vma=False
    )
```

```python
import functools

import jax
import jax.numpy as jnp
from jax import lax
from jax.experimental import pallas as pl
from jax.experimental.pallas import tpu as pltpu
from jax.sharding import PartitionSpec as P

HD = 128
BLOCK = 512
NEG = -1e30
PARTS = 8
MESH = pl.DeviceIdType.MESH
SCALE2 = 1.4426950408889634 / HD**0.5


def kernel(
    n_ctx, n_tp, heads,
    q_hbm, k_hbm, v_hbm, sel_ref, w_ref, out_ref,
    *scratch,
):
    kv = scratch[:heads]
    stage = scratch[heads:2 * heads]
    (q_ref, wbuf, att, acc, up_send, up_recv, sib_send, sib_recv, w_send, w_recv,
     ws_send, ws_recv, att_send, att_recv, in_sem) = scratch[2 * heads:]
    chips = n_ctx // 2
    group = heads // 2
    gk = group * HD
    cols = out_ref.shape[1]
    ctx = lax.axis_index("ctx")
    tp = lax.axis_index("tp")
    z, c = ctx // 2, ctx % 2
    sib = z * 2 + 1 - c
    above, below = ctx + 2, ctx - 2
    not_last = z < chips - 1
    chained = z < chips - 2
    packs = z == chips - 2

    def load_q():
        return pltpu.make_async_copy(q_hbm, q_ref, in_sem.at[2, 0])

    def load_kv(h, part):
        src = (k_hbm, v_hbm)[part].at[:, h * HD:(h + 1) * HD]
        return pltpu.make_async_copy(src, kv[h].at[ctx, part], in_sem.at[part, h])

    for h in range(heads):
        load_kv(h, 0).start()
        load_kv(h, 1).start()
    load_q().start()

    barrier = pltpu.get_barrier_semaphore()

    def greet(**where):
        pl.semaphore_signal(barrier, inc=1, device_id=where, device_id_type=MESH)

    greet(ctx=sib)
    for d in range(1, n_tp):
        greet(tp=(tp + d) % n_tp)

    @pl.when(not_last)
    def _():
        greet(ctx=above)

    @pl.when(z > 0)
    def _():
        greet(ctx=below)

    ends = (z == 0).astype(jnp.int32) + (z == chips - 1).astype(jnp.int32)
    pl.semaphore_wait(barrier, n_tp + 2 - ends)

    def remote(src, dst, send, recv, **where):
        return pltpu.make_async_remote_copy(
            src_ref=src, dst_ref=dst, send_sem=send, recv_sem=recv,
            device_id=where, device_id_type=MESH,
        )

    def up(h, zz):
        slot = kv[h].at[zz * 2 + c]
        return remote(slot, slot, up_send.at[h, zz], up_recv.at[h, zz], ctx=above)

    def from_below(h, zz):
        slot = kv[h].at[zz * 2 + c]
        return remote(slot, slot, up_send.at[h, zz], up_recv.at[h, zz], ctx=below)

    def side(h, zz):
        slot = kv[h].at[zz * 2 + c]
        return remote(slot, slot, sib_send.at[h, zz], sib_recv.at[h, zz], ctx=sib)

    def from_side(h, zz):
        slot = kv[h].at[zz * 2 + 1 - c]
        return remote(slot, slot, sib_send.at[h, zz], sib_recv.at[h, zz], ctx=sib)

    def send_on(h, zz):
        @pl.when(chained)
        def _():
            up(h, zz).start()

        side(h, zz).start()

    def packed(h, where):
        return remote(stage[h], kv[h].at[pl.ds(0, 2)], up_send.at[h, 0], up_recv.at[h, 0], ctx=where)

    def pack(h):
        for slot in range(2):
            want = sel_ref[slot + 1, above]
            stage[h][slot] = kv[h][jnp.where(want < 2 * (z + 1), want, ctx)]
        packed(h, above).start()

    def w_rows(half, p):
        return wbuf.at[half, pl.ds(pl.multiple_of(p * gk, gk), gk)]

    def w_out(p):
        src = w_ref.at[pl.ds(pl.multiple_of(c * gk, gk), gk), pl.ds(pl.multiple_of(p * cols, 128), cols)]
        return remote(src, w_rows(c, tp), w_send.at[p], w_recv.at[tp], tp=p)

    def w_in(p):
        return remote(w_rows(c, p), w_rows(c, p), w_send.at[p], w_recv.at[p], tp=p)

    def w_side(p):
        return remote(w_rows(c, p), w_rows(c, p), ws_send.at[p], ws_recv.at[p], ctx=sib)

    def w_from_side(p):
        return remote(w_rows(1 - c, p), w_rows(1 - c, p), ws_send.at[p], ws_recv.at[p], ctx=sib)

    def w_own(half):
        src = w_ref.at[half * gk:(half + 1) * gk, pl.ds(pl.multiple_of(tp * cols, 128), cols)]
        sem = w_send if half == 0 else ws_send
        return pltpu.make_async_copy(src, w_rows(half, tp), sem.at[tp])

    def att_slot(h, p):
        start = p * gk + (h % group) * HD
        return att.at[h // group, :, pl.ds(pl.multiple_of(start, HD), HD)]

    def att_out(h, p):
        return remote(att_slot(h, tp), att_slot(h, tp), att_send.at[h, p], att_recv.at[h, tp], tp=p)

    def att_in(h, p):
        return remote(att_slot(h, p), att_slot(h, p), att_send.at[h, p], att_recv.at[h, p], tp=p)

    peers = [(tp + d) % n_tp for d in range(1, n_tp)]

    def own_block(h):
        load_kv(h, 0).wait()
        load_kv(h, 1).wait()
        send_on(h, z)

    own_block(0)
    for p in peers:
        w_out(p).start()
    w_own(0).start()
    w_own(1).start()

    first, second = sel_ref[1, ctx], sel_ref[2, ctx]
    bias1 = jnp.where(first == ctx, jnp.float32(NEG), jnp.float32(0))
    bias2 = jnp.where(second == ctx, jnp.float32(NEG), jnp.float32(0))
    near = jnp.where(not_last, 0, 2 * z)
    first = jnp.where(first >= near, first, 0)
    second = jnp.where(second >= near, second, 1)
    contract = (((1,), (1,)), ((), ()))

    def attend(h):
        rows = 256
        k1, v1 = kv[h][first, 0], kv[h][first, 1]
        k2, v2 = kv[h][second, 0], kv[h][second, 1]
        for r in range(BLOCK // rows):
            depth = (r + 1) * rows
            q = q_ref[r * rows:(r + 1) * rows, h * HD:(h + 1) * HD]
            k0 = kv[h][ctx, 0, :depth]
            v0 = kv[h][ctx, 1, :depth]

            def score(k):
                return lax.dot_general(q, k, contract, preferred_element_type=jnp.float32)

            s0, s1, s2 = score(k0), score(k1) + bias1, score(k2) + bias2
            rid = lax.broadcasted_iota(jnp.int32, s0.shape, 0) + r * rows
            cid = lax.broadcasted_iota(jnp.int32, s0.shape, 1)
            s0 = jnp.where(cid <= rid, s0, NEG)
            top = jnp.maximum(
                jnp.max(s0, axis=1, keepdims=True),
                jnp.maximum(jnp.max(s1, axis=1, keepdims=True), jnp.max(s2, axis=1, keepdims=True)),
            )
            e0, e1, e2 = (jnp.exp2((s - top) * SCALE2) for s in (s0, s1, s2))
            total = (
                jnp.sum(e0, axis=1, keepdims=True)
                + jnp.sum(e1, axis=1, keepdims=True)
                + jnp.sum(e2, axis=1, keepdims=True)
            )
            numer = sum(
                jnp.dot(e.astype(jnp.bfloat16), v, preferred_element_type=jnp.float32)
                for e, v in ((e0, v0), (e1, v1), (e2, v2))
            )
            start = pl.multiple_of(tp * gk + (h % group) * HD, HD)
            att[h // group, r * rows:(r + 1) * rows, pl.ds(start, HD)] = (numer / total).astype(jnp.bfloat16)
        for p in peers:
            att_out(h, p).start()

    tile = 256 if cols % 256 == 0 else 128

    def project(g):
        for h in range(g * group, (g + 1) * group):
            for p in peers:
                att_in(h, p).wait_recv()

        @pl.loop(0, cols // tile)
        def _(n):
            at = pl.ds(pl.multiple_of(n * tile, tile), tile)
            part = jnp.dot(att[g], wbuf[g, :, at], preferred_element_type=jnp.float32)
            if g == 0:
                acc[:, at] = part
            else:
                out_ref[:, at] = (acc[:, at] + part).astype(out_ref.dtype)

    def first_half():
        for p in peers:
            w_in(p).wait_recv()
            w_side(p).start()
        w_own(0).wait()
        w_own(1).wait()
        for p in peers:
            w_from_side(p).wait_recv()
        project(0)

    load_q().wait()
    for h in range(heads):
        if h + 1 < heads:
            own_block(h + 1)
        if h == heads - 1:
            pl.when(z == chips - 1)(first_half)

        @pl.when(not_last)
        def _():
            @pl.loop(0, z)
            def _(s):
                zz = z - 1 - s
                from_below(h, zz).wait_recv()
                send_on(h, zz)

            @pl.loop(0, z)
            def _(zz):
                from_side(h, zz).wait_recv()

        from_side(h, z).wait_recv()

        @pl.when(packs)
        def _():
            pack(h)

        @pl.when(z == chips - 1)
        def _():
            packed(h, below).wait_recv()

        attend(h)
    pl.when(not_last)(first_half)
    project(1)

    for h in range(heads):
        side(h, z).wait_send()

        @pl.when(not_last)
        def _():
            @pl.loop(0, z)
            def _(zz):
                side(h, zz).wait_send()

        @pl.when(chained)
        def _():
            @pl.loop(0, z + 1)
            def _(zz):
                up(h, zz).wait_send()

        @pl.when(packs)
        def _():
            packed(h, above).wait_send()

        for p in peers:
            att_out(h, p).wait_send()
    for p in peers:
        w_out(p).wait_send()
        w_side(p).wait_send()


def hand_over(src, dst, sem):
    step = src.shape[0] // PARTS
    copies = [
        pltpu.make_async_copy(src.at[n * step:(n + 1) * step], dst.at[n * step:(n + 1) * step], sem.at[n])
        for n in range(PARTS)
    ]
    for copy in copies:
        copy.start()
    for copy in copies:
        copy.wait()


def per_device(n_ctx, n_tp, queries, key_rows, value_rows, selection, out_weight):
    rows, width = queries.shape
    heads = width // HD
    cols = out_weight.shape[1] // n_tp
    gk = heads // 2 * HD
    chips = n_ctx // 2
    vmem = pl.BlockSpec(memory_space=pltpu.VMEM)
    hbm = pl.BlockSpec(memory_space=pl.ANY)
    dma = pltpu.SemaphoreType.DMA
    held = pl.pallas_call(
        functools.partial(kernel, n_ctx, n_tp, heads),
        out_shape=jax.ShapeDtypeStruct((rows, cols), jnp.bfloat16),
        in_specs=[
            hbm, hbm, hbm,
            pl.BlockSpec(memory_space=pltpu.SMEM),
            hbm,
        ],
        out_specs=vmem,
        scratch_shapes=[pltpu.VMEM((n_ctx, 2, BLOCK, HD), jnp.bfloat16) for _ in range(heads)]
        + [pltpu.VMEM((2, 2, BLOCK, HD), jnp.bfloat16) for _ in range(heads)] + [
            pltpu.VMEM((rows, width), jnp.bfloat16),
            pltpu.VMEM((2, n_tp * gk, cols), jnp.bfloat16),
            pltpu.VMEM((2, rows, n_tp * gk), jnp.bfloat16),
            pltpu.VMEM((rows, cols), jnp.float32),
            dma((heads, chips)), dma((heads, chips)),
            dma((heads, chips)), dma((heads, chips)),
            dma((n_tp,)), dma((n_tp,)), dma((n_tp,)), dma((n_tp,)),
            dma((heads, n_tp)), dma((heads, n_tp)),
            dma((3, heads)),
        ],
        compiler_params=pltpu.CompilerParams(
            collective_id=0, has_side_effects=True, vmem_limit_bytes=52 * 2**20
        ),
        cost_estimate=pl.CostEstimate(
            flops=2 * rows * cols * n_tp * width + 12 * rows * BLOCK * width,
            bytes_accessed=2 * (out_weight.size + 4 * rows * width),
            transcendentals=3 * rows * BLOCK * heads,
        ),
    )(queries, key_rows, value_rows, selection.T, out_weight)
    return pl.pallas_call(
        hand_over,
        out_shape=jax.ShapeDtypeStruct((rows, cols), jnp.bfloat16),
        in_specs=[hbm],
        out_specs=hbm,
        scratch_shapes=[dma((PARTS,))],
    )(held)


def solution(mesh):
    placed = (P("ctx", "tp"), P("ctx", "tp"), P("ctx", "tp"), P(), P("tp", None))
    body = functools.partial(per_device, mesh.shape["ctx"], mesh.shape["tp"])
    return jax.shard_map(
        body, mesh=mesh, in_specs=placed, out_specs=P("ctx", "tp"), check_vma=False
    )
```

```python
import functools

import jax
import jax.numpy as jnp
from jax import lax
from jax.experimental import pallas as pl
from jax.experimental.pallas import tpu as pltpu
from jax.sharding import PartitionSpec as P

HD = 128
BLOCK = 512
NEG = -1e30
PARTS = 8
MESH = pl.DeviceIdType.MESH
SCALE2 = 1.4426950408889634 / HD**0.5


def kernel(
    n_ctx, n_tp, heads,
    q_hbm, k_hbm, v_hbm, sel_ref, w_ref, out_ref,
    *scratch,
):
    units = 2 * heads
    kv = scratch[:units]
    stage = scratch[units:2 * units]
    (q_ref, wbuf, att, acc, up_send, up_recv, sib_send, sib_recv, w_send, w_recv,
     ws_send, ws_recv, att_send, att_recv, in_sem) = scratch[2 * units:]
    chips = n_ctx // 2
    group = heads // 2
    gk = group * HD
    cols = out_ref.shape[1]
    ctx = lax.axis_index("ctx")
    tp = lax.axis_index("tp")
    z, c = ctx // 2, ctx % 2
    sib = z * 2 + 1 - c
    above, below = ctx + 2, ctx - 2
    not_last = z < chips - 1
    chained = z < chips - 2
    packs = z == chips - 2

    def load_q():
        return pltpu.make_async_copy(q_hbm, q_ref, in_sem.at[2, 0])

    def load_kv(h, part):
        src = (k_hbm, v_hbm)[part].at[:, h * HD:(h + 1) * HD]
        return pltpu.make_async_copy(src, kv[2 * h + part].at[ctx], in_sem.at[part, h])

    for h in range(heads):
        load_kv(h, 0).start()
        load_kv(h, 1).start()
    load_q().start()

    barrier = pltpu.get_barrier_semaphore()

    def greet(**where):
        pl.semaphore_signal(barrier, inc=1, device_id=where, device_id_type=MESH)

    greet(ctx=sib)
    for d in range(1, n_tp):
        greet(tp=(tp + d) % n_tp)

    @pl.when(not_last)
    def _():
        greet(ctx=above)

    @pl.when(z > 0)
    def _():
        greet(ctx=below)

    ends = (z == 0).astype(jnp.int32) + (z == chips - 1).astype(jnp.int32)
    pl.semaphore_wait(barrier, n_tp + 2 - ends)

    def remote(src, dst, send, recv, **where):
        return pltpu.make_async_remote_copy(
            src_ref=src, dst_ref=dst, send_sem=send, recv_sem=recv,
            device_id=where, device_id_type=MESH,
        )

    def up(u, zz):
        slot = kv[u].at[zz * 2 + c]
        return remote(slot, slot, up_send.at[u, zz], up_recv.at[u, zz], ctx=above)

    def from_below(u, zz):
        slot = kv[u].at[zz * 2 + c]
        return remote(slot, slot, up_send.at[u, zz], up_recv.at[u, zz], ctx=below)

    def side(u, zz):
        slot = kv[u].at[zz * 2 + c]
        return remote(slot, slot, sib_send.at[u, zz], sib_recv.at[u, zz], ctx=sib)

    def from_side(u, zz):
        slot = kv[u].at[zz * 2 + 1 - c]
        return remote(slot, slot, sib_send.at[u, zz], sib_recv.at[u, zz], ctx=sib)

    def send_on(u, zz):
        @pl.when(chained)
        def _():
            up(u, zz).start()

        side(u, zz).start()

    def packed(u, where):
        return remote(stage[u], kv[u].at[pl.ds(0, 2)], up_send.at[u, 0], up_recv.at[u, 0], ctx=where)

    def pack(u):
        for slot in range(2):
            want = sel_ref[slot + 1, above]
            stage[u][slot] = kv[u][jnp.where(want < 2 * (z + 1), want, ctx)]
        packed(u, above).start()

    def w_rows(half, p):
        return wbuf.at[half, pl.ds(pl.multiple_of(p * gk, gk), gk)]

    def w_out(p):
        src = w_ref.at[pl.ds(pl.multiple_of(c * gk, gk), gk), pl.ds(pl.multiple_of(p * cols, 128), cols)]
        return remote(src, w_rows(c, tp), w_send.at[p], w_recv.at[tp], tp=p)

    def w_in(p):
        return remote(w_rows(c, p), w_rows(c, p), w_send.at[p], w_recv.at[p], tp=p)

    def w_side(p):
        return remote(w_rows(c, p), w_rows(c, p), ws_send.at[p], ws_recv.at[p], ctx=sib)

    def w_from_side(p):
        return remote(w_rows(1 - c, p), w_rows(1 - c, p), ws_send.at[p], ws_recv.at[p], ctx=sib)

    def w_own(half):
        src = w_ref.at[half * gk:(half + 1) * gk, pl.ds(pl.multiple_of(tp * cols, 128), cols)]
        sem = w_send if half == 0 else ws_send
        return pltpu.make_async_copy(src, w_rows(half, tp), sem.at[tp])

    def att_slot(h, p):
        start = p * gk + (h % group) * HD
        return att.at[h // group, :, pl.ds(pl.multiple_of(start, HD), HD)]

    def att_out(h, p):
        return remote(att_slot(h, tp), att_slot(h, tp), att_send.at[h, p], att_recv.at[h, tp], tp=p)

    def att_in(h, p):
        return remote(att_slot(h, p), att_slot(h, p), att_send.at[h, p], att_recv.at[h, p], tp=p)

    relay = n_tp == 4
    if relay:
        tx, ty = tp % 2, tp // 2
        px, py, pd = ty * 2 + 1 - tx, (1 - ty) * 2 + tx, (1 - ty) * 2 + 1 - tx
        peers = [px, py, pd]
    else:
        peers = [(tp + d) % n_tp for d in range(1, n_tp)]

    def relayed(h):
        return relay and h < heads - 1

    def att_relay(h):
        owner, target = (px, py) if h % 2 == 0 else (py, px)
        return remote(att_slot(h, owner), att_slot(h, owner), att_send.at[h, pd], att_recv.at[h, owner], tp=target)

    def pass_on(h):
        if relayed(h):
            att_in(h, px if h % 2 == 0 else py).wait_recv()
            att_relay(h).start()

    def await_att(h, n):
        if not (relayed(h) and n == h % 2):
            att_in(h, peers[n]).wait_recv()

    def own_block(u):
        load_kv(u // 2, u % 2).wait()
        send_on(u, z)

    own_block(0)
    own_block(1)
    for p in peers:
        w_out(p).start()
    w_own(0).start()
    w_own(1).start()

    first, second = sel_ref[1, ctx], sel_ref[2, ctx]
    bias1 = jnp.where(first == ctx, jnp.float32(NEG), jnp.float32(0))
    bias2 = jnp.where(second == ctx, jnp.float32(NEG), jnp.float32(0))
    near = jnp.where(not_last, 0, 2 * z)
    first = jnp.where(first >= near, first, 0)
    second = jnp.where(second >= near, second, 1)
    contract = (((1,), (1,)), ((), ()))

    def attend(h):
        rows = 256
        k1, v1 = kv[2 * h][first], kv[2 * h + 1][first]
        k2, v2 = kv[2 * h][second], kv[2 * h + 1][second]
        for r in range(BLOCK // rows):
            depth = (r + 1) * rows
            q = q_ref[r * rows:(r + 1) * rows, h * HD:(h + 1) * HD]
            k0 = kv[2 * h][ctx, :depth]
            v0 = kv[2 * h + 1][ctx, :depth]

            def score(k):
                return lax.dot_general(q, k, contract, preferred_element_type=jnp.float32)

            s0, s1, s2 = score(k0), score(k1) + bias1, score(k2) + bias2
            rid = lax.broadcasted_iota(jnp.int32, s0.shape, 0) + r * rows
            cid = lax.broadcasted_iota(jnp.int32, s0.shape, 1)
            s0 = jnp.where(cid <= rid, s0, NEG)
            top = jnp.maximum(
                jnp.max(s0, axis=1, keepdims=True),
                jnp.maximum(jnp.max(s1, axis=1, keepdims=True), jnp.max(s2, axis=1, keepdims=True)),
            )
            e0, e1, e2 = (jnp.exp2((s - top) * SCALE2) for s in (s0, s1, s2))
            total = (
                jnp.sum(e0, axis=1, keepdims=True)
                + jnp.sum(e1, axis=1, keepdims=True)
                + jnp.sum(e2, axis=1, keepdims=True)
            )
            numer = sum(
                jnp.dot(e.astype(jnp.bfloat16), v, preferred_element_type=jnp.float32)
                for e, v in ((e0, v0), (e1, v1), (e2, v2))
            )
            start = pl.multiple_of(tp * gk + (h % group) * HD, HD)
            att[h // group, r * rows:(r + 1) * rows, pl.ds(start, HD)] = (numer / total).astype(jnp.bfloat16)
        for p in peers[:2] if relayed(h) else peers:
            att_out(h, p).start()

    tile = 256 if cols % 256 == 0 else 128

    def project(g):
        for h in range(g * group, (g + 1) * group):
            for n in range(n_tp - 1):
                await_att(h, n)

        @pl.loop(0, cols // tile)
        def _(n):
            at = pl.ds(pl.multiple_of(n * tile, tile), tile)
            part = jnp.dot(att[g], wbuf[g, :, at], preferred_element_type=jnp.float32)
            if g == 0:
                acc[:, at] = part
            else:
                out_ref[:, at] = (acc[:, at] + part).astype(out_ref.dtype)

    def first_half():
        for p in peers:
            w_in(p).wait_recv()
            w_side(p).start()
        w_own(0).wait()
        w_own(1).wait()
        for p in peers:
            w_from_side(p).wait_recv()
        project(0)

    def add_rows(p, opening=False, closing=False):
        at_p = pl.ds(pl.multiple_of(p * gk, gk), gk)

        @pl.loop(0, cols // tile)
        def _(n):
            at = pl.ds(pl.multiple_of(n * tile, tile), tile)
            part = sum(
                jnp.dot(att[g, :, at_p], wbuf[g, at_p, at], preferred_element_type=jnp.float32)
                for g in range(2)
            )
            if not opening:
                part = part + acc[:, at]
            if closing:
                out_ref[:, at] = part.astype(out_ref.dtype)
            else:
                acc[:, at] = part

    def by_peer():
        for h in range(heads):
            pass_on(h)
        w_own(0).wait()
        w_own(1).wait()

        def add_peer(n):
            w_from_side(peers[n]).wait_recv()
            for h in range(heads):
                await_att(h, n)
            add_rows(peers[n], closing=n == n_tp - 2)

        for n in range(n_tp - 1):
            w_in(peers[n]).wait_recv()
            w_side(peers[n]).start()
            if n == 0:
                add_rows(tp, opening=True)
            else:
                add_peer(n - 1)
        add_peer(n_tp - 2)

    is_last = z == chips - 1
    load_q().wait()
    for u in range(units):
        h = u // 2
        if u + 2 < units:
            own_block(u + 2)
        if u == units - 2:
            pl.when(is_last)(first_half)

        @pl.when(not_last)
        def _():
            @pl.loop(0, z)
            def _(s):
                zz = z - 1 - s
                from_below(u, zz).wait_recv()
                send_on(u, zz)

            @pl.loop(0, z)
            def _(zz):
                from_side(u, zz).wait_recv()

        from_side(u, z).wait_recv()

        @pl.when(packs)
        def _():
            pack(u)

        @pl.when(is_last)
        def _():
            packed(u, below).wait_recv()

        if u % 2 == 1:
            if h >= 1:
                pl.when(is_last)(functools.partial(pass_on, h - 1))
            attend(h)
    pl.when(is_last)(functools.partial(project, 1))
    pl.when(not_last)(by_peer)

    for u in range(units):
        side(u, z).wait_send()

        @pl.when(not_last)
        def _():
            @pl.loop(0, z)
            def _(zz):
                side(u, zz).wait_send()

        @pl.when(chained)
        def _():
            @pl.loop(0, z + 1)
            def _(zz):
                up(u, zz).wait_send()

        @pl.when(packs)
        def _():
            packed(u, above).wait_send()

    for h in range(heads):
        for p in peers[:2] if relayed(h) else peers:
            att_out(h, p).wait_send()
        if relayed(h):
            att_relay(h).wait_send()
    for p in peers:
        w_out(p).wait_send()
        w_side(p).wait_send()


def hand_over(src, dst):
    dst[...] = src[...]


def per_device(n_ctx, n_tp, queries, key_rows, value_rows, selection, out_weight):
    rows, width = queries.shape
    heads = width // HD
    cols = out_weight.shape[1] // n_tp
    gk = heads // 2 * HD
    chips = n_ctx // 2
    vmem = pl.BlockSpec(memory_space=pltpu.VMEM)
    hbm = pl.BlockSpec(memory_space=pltpu.HBM)
    dma = pltpu.SemaphoreType.DMA
    held = pl.pallas_call(
        functools.partial(kernel, n_ctx, n_tp, heads),
        out_shape=jax.ShapeDtypeStruct((rows, cols), jnp.bfloat16),
        in_specs=[
            hbm, hbm, hbm,
            pl.BlockSpec(memory_space=pltpu.SMEM),
            hbm,
        ],
        out_specs=vmem,
        scratch_shapes=[pltpu.VMEM((n_ctx, BLOCK, HD), jnp.bfloat16) for _ in range(2 * heads)]
        + [pltpu.VMEM((2, BLOCK, HD), jnp.bfloat16) for _ in range(2 * heads)] + [
            pltpu.VMEM((rows, width), jnp.bfloat16),
            pltpu.VMEM((2, n_tp * gk, cols), jnp.bfloat16),
            pltpu.VMEM((2, rows, n_tp * gk), jnp.bfloat16),
            pltpu.VMEM((rows, cols), jnp.float32),
            dma((2 * heads, chips)), dma((2 * heads, chips)),
            dma((2 * heads, chips)), dma((2 * heads, chips)),
            dma((n_tp,)), dma((n_tp,)), dma((n_tp,)), dma((n_tp,)),
            dma((heads, n_tp)), dma((heads, n_tp)),
            dma((3, heads)),
        ],
        compiler_params=pltpu.CompilerParams(
            collective_id=0, has_side_effects=True, vmem_limit_bytes=63 * 2**20
        ),
        cost_estimate=pl.CostEstimate(
            flops=2 * rows * cols * n_tp * width + 12 * rows * BLOCK * width,
            bytes_accessed=2 * (out_weight.size + 4 * rows * width),
            transcendentals=3 * rows * BLOCK * heads,
        ),
    )(queries, key_rows, value_rows, selection.T, out_weight)
    return pl.pallas_call(
        hand_over,
        out_shape=jax.ShapeDtypeStruct((rows, cols), jnp.bfloat16),
        grid=(PARTS,),
        in_specs=[pl.BlockSpec((rows // PARTS, cols), lambda n: (n, 0))],
        out_specs=pl.BlockSpec((rows // PARTS, cols), lambda n: (n, 0)),
    )(held)


def solution(mesh):
    placed = (P("ctx", "tp"), P("ctx", "tp"), P("ctx", "tp"), P(), P("tp", None))
    body = functools.partial(per_device, mesh.shape["ctx"], mesh.shape["tp"])
    return jax.shard_map(
        body, mesh=mesh, in_specs=placed, out_specs=P("ctx", "tp"), check_vma=False
    )
```

```python
import functools

import jax
import jax.numpy as jnp
from jax import lax
from jax.experimental import pallas as pl
from jax.experimental.pallas import tpu as pltpu
from jax.sharding import PartitionSpec as P

HD = 128
BLOCK = 512
NEG = -1e30
MESH = pl.DeviceIdType.MESH
SCALE2 = 1.4426950408889634 / HD**0.5


def kernel(
    n_ctx, n_tp, heads,
    q_hbm, k_hbm, v_hbm, sel_ref, w_ref, out_ref,
    *scratch,
):
    kv = scratch[:heads]
    stage = scratch[heads:2 * heads]
    (q_ref, wbuf, att, acc, up_send, up_recv, sib_send, sib_recv, w_send, w_recv,
     ws_send, ws_recv, att_send, att_recv, in_sem) = scratch[2 * heads:]
    chips = n_ctx // 2
    group = heads // 2
    gk = group * HD
    cols = out_ref.shape[1]
    ctx = lax.axis_index("ctx")
    tp = lax.axis_index("tp")
    z, c = ctx // 2, ctx % 2
    sib = z * 2 + 1 - c
    above, below = ctx + 2, ctx - 2
    not_last = z < chips - 1
    chained = z < chips - 2
    packs = z == chips - 2

    def load_q():
        return pltpu.make_async_copy(q_hbm, q_ref, in_sem.at[2, 0])

    def load_kv(h, part):
        src = (k_hbm, v_hbm)[part].at[:, h * HD:(h + 1) * HD]
        return pltpu.make_async_copy(src, kv[h].at[ctx, part], in_sem.at[part, h])

    for h in range(heads):
        load_kv(h, 0).start()
        load_kv(h, 1).start()
    load_q().start()

    barrier = pltpu.get_barrier_semaphore()

    def greet(**where):
        pl.semaphore_signal(barrier, inc=1, device_id=where, device_id_type=MESH)

    greet(ctx=sib)
    for d in range(1, n_tp):
        greet(tp=(tp + d) % n_tp)

    @pl.when(not_last)
    def _():
        greet(ctx=above)

    @pl.when(z > 0)
    def _():
        greet(ctx=below)

    ends = (z == 0).astype(jnp.int32) + (z == chips - 1).astype(jnp.int32)
    pl.semaphore_wait(barrier, n_tp + 2 - ends)

    def remote(src, dst, send, recv, **where):
        return pltpu.make_async_remote_copy(
            src_ref=src, dst_ref=dst, send_sem=send, recv_sem=recv,
            device_id=where, device_id_type=MESH,
        )

    def up(h, zz):
        slot = kv[h].at[zz * 2 + c]
        return remote(slot, slot, up_send.at[h, zz], up_recv.at[h, zz], ctx=above)

    def from_below(h, zz):
        slot = kv[h].at[zz * 2 + c]
        return remote(slot, slot, up_send.at[h, zz], up_recv.at[h, zz], ctx=below)

    def side(h, zz):
        slot = kv[h].at[zz * 2 + c]
        return remote(slot, slot, sib_send.at[h, zz], sib_recv.at[h, zz], ctx=sib)

    def from_side(h, zz):
        slot = kv[h].at[zz * 2 + 1 - c]
        return remote(slot, slot, sib_send.at[h, zz], sib_recv.at[h, zz], ctx=sib)

    def send_on(h, zz):
        @pl.when(chained)
        def _():
            up(h, zz).start()

        side(h, zz).start()

    def packed(h, where):
        return remote(stage[h], kv[h].at[pl.ds(0, 2)], up_send.at[h, 0], up_recv.at[h, 0], ctx=where)

    def pack(h):
        for slot in range(2):
            want = sel_ref[slot + 1, above]
            stage[h][slot] = kv[h][jnp.where(want < 2 * (z + 1), want, ctx)]
        packed(h, above).start()

    def w_rows(half, p):
        return wbuf.at[half, pl.ds(pl.multiple_of(p * gk, gk), gk)]

    def w_out(p):
        src = w_ref.at[pl.ds(pl.multiple_of(c * gk, gk), gk), pl.ds(pl.multiple_of(p * cols, 128), cols)]
        return remote(src, w_rows(c, tp), w_send.at[p], w_recv.at[tp], tp=p)

    def w_in(p):
        return remote(w_rows(c, p), w_rows(c, p), w_send.at[p], w_recv.at[p], tp=p)

    def w_side(p):
        return remote(w_rows(c, p), w_rows(c, p), ws_send.at[p], ws_recv.at[p], ctx=sib)

    def w_from_side(p):
        return remote(w_rows(1 - c, p), w_rows(1 - c, p), ws_send.at[p], ws_recv.at[p], ctx=sib)

    def w_own(half):
        src = w_ref.at[half * gk:(half + 1) * gk, pl.ds(pl.multiple_of(tp * cols, 128), cols)]
        sem = w_send if half == 0 else ws_send
        return pltpu.make_async_copy(src, w_rows(half, tp), sem.at[tp])

    def att_slot(h, p):
        start = p * gk + (h % group) * HD
        return att.at[h // group, :, pl.ds(pl.multiple_of(start, HD), HD)]

    def att_out(h, p):
        return remote(att_slot(h, tp), att_slot(h, tp), att_send.at[h, p], att_recv.at[h, tp], tp=p)

    def att_in(h, p):
        return remote(att_slot(h, p), att_slot(h, p), att_send.at[h, p], att_recv.at[h, p], tp=p)

    peers = [(tp + d) % n_tp for d in range(1, n_tp)]

    def own_block(h):
        load_kv(h, 0).wait()
        load_kv(h, 1).wait()
        send_on(h, z)

    own_block(0)
    for p in peers:
        w_out(p).start()
    w_own(0).start()
    w_own(1).start()

    first, second = sel_ref[1, ctx], sel_ref[2, ctx]
    bias1 = jnp.where(first == ctx, jnp.float32(NEG), jnp.float32(0))
    bias2 = jnp.where(second == ctx, jnp.float32(NEG), jnp.float32(0))
    near = jnp.where(not_last, 0, 2 * z)
    first = jnp.where(first >= near, first, 0)
    second = jnp.where(second >= near, second, 1)
    contract = (((1,), (1,)), ((), ()))

    def attend(h):
        rows = 256
        k1, v1 = kv[h][first, 0], kv[h][first, 1]
        k2, v2 = kv[h][second, 0], kv[h][second, 1]
        for r in range(BLOCK // rows):
            depth = (r + 1) * rows
            q = q_ref[r * rows:(r + 1) * rows, h * HD:(h + 1) * HD]
            k0 = kv[h][ctx, 0, :depth]
            v0 = kv[h][ctx, 1, :depth]

            def score(k):
                return lax.dot_general(q, k, contract, preferred_element_type=jnp.float32)

            s0, s1, s2 = score(k0), score(k1) + bias1, score(k2) + bias2
            rid = lax.broadcasted_iota(jnp.int32, s0.shape, 0) + r * rows
            cid = lax.broadcasted_iota(jnp.int32, s0.shape, 1)
            s0 = jnp.where(cid <= rid, s0, NEG)
            top = jnp.maximum(
                jnp.max(s0, axis=1, keepdims=True),
                jnp.maximum(jnp.max(s1, axis=1, keepdims=True), jnp.max(s2, axis=1, keepdims=True)),
            )
            e0, e1, e2 = (jnp.exp2((s - top) * SCALE2) for s in (s0, s1, s2))
            total = (
                jnp.sum(e0, axis=1, keepdims=True)
                + jnp.sum(e1, axis=1, keepdims=True)
                + jnp.sum(e2, axis=1, keepdims=True)
            )
            numer = sum(
                jnp.dot(e.astype(jnp.bfloat16), v, preferred_element_type=jnp.float32)
                for e, v in ((e0, v0), (e1, v1), (e2, v2))
            )
            start = pl.multiple_of(tp * gk + (h % group) * HD, HD)
            att[h // group, r * rows:(r + 1) * rows, pl.ds(start, HD)] = (numer / total).astype(jnp.bfloat16)
        for p in peers:
            att_out(h, p).start()

    tile = 256 if cols % 256 == 0 else 128

    def project(g):
        for h in range(g * group, (g + 1) * group):
            for p in peers:
                att_in(h, p).wait_recv()

        @pl.loop(0, cols // tile)
        def _(n):
            at = pl.ds(pl.multiple_of(n * tile, tile), tile)
            part = jnp.dot(att[g], wbuf[g, :, at], preferred_element_type=jnp.float32)
            if g == 0:
                acc[:, at] = part
            else:
                out_ref[:, at] = (acc[:, at] + part).astype(out_ref.dtype)

    def first_half():
        for p in peers:
            w_in(p).wait_recv()
            w_side(p).start()
        w_own(0).wait()
        w_own(1).wait()
        for p in peers:
            w_from_side(p).wait_recv()
        project(0)

    load_q().wait()
    for h in range(heads):
        if h + 1 < heads:
            own_block(h + 1)
        if h == heads - 1:
            pl.when(z == chips - 1)(first_half)

        @pl.when(not_last)
        def _():
            @pl.loop(0, z)
            def _(s):
                zz = z - 1 - s
                from_below(h, zz).wait_recv()
                send_on(h, zz)

            @pl.loop(0, z)
            def _(zz):
                from_side(h, zz).wait_recv()

        from_side(h, z).wait_recv()

        @pl.when(packs)
        def _():
            pack(h)

        @pl.when(z == chips - 1)
        def _():
            packed(h, below).wait_recv()

        attend(h)
    pl.when(not_last)(first_half)
    project(1)

    for h in range(heads):
        side(h, z).wait_send()

        @pl.when(not_last)
        def _():
            @pl.loop(0, z)
            def _(zz):
                side(h, zz).wait_send()

        @pl.when(chained)
        def _():
            @pl.loop(0, z + 1)
            def _(zz):
                up(h, zz).wait_send()

        @pl.when(packs)
        def _():
            packed(h, above).wait_send()

        for p in peers:
            att_out(h, p).wait_send()
    for p in peers:
        w_out(p).wait_send()
        w_side(p).wait_send()


def per_device(n_ctx, n_tp, queries, key_rows, value_rows, selection, out_weight):
    rows, width = queries.shape
    heads = width // HD
    cols = out_weight.shape[1] // n_tp
    gk = heads // 2 * HD
    chips = n_ctx // 2
    vmem = pl.BlockSpec(memory_space=pltpu.VMEM)
    hbm = pl.BlockSpec(memory_space=pl.ANY)
    dma = pltpu.SemaphoreType.DMA
    return pl.pallas_call(
        functools.partial(kernel, n_ctx, n_tp, heads),
        out_shape=jax.ShapeDtypeStruct((rows, cols), jnp.bfloat16),
        in_specs=[
            hbm, hbm, hbm,
            pl.BlockSpec(memory_space=pltpu.SMEM),
            hbm,
        ],
        out_specs=vmem,
        scratch_shapes=[pltpu.VMEM((n_ctx, 2, BLOCK, HD), jnp.bfloat16) for _ in range(heads)]
        + [pltpu.VMEM((2, 2, BLOCK, HD), jnp.bfloat16) for _ in range(heads)] + [
            pltpu.VMEM((rows, width), jnp.bfloat16),
            pltpu.VMEM((2, n_tp * gk, cols), jnp.bfloat16),
            pltpu.VMEM((2, rows, n_tp * gk), jnp.bfloat16),
            pltpu.VMEM((rows, cols), jnp.float32),
            dma((heads, chips)), dma((heads, chips)),
            dma((heads, chips)), dma((heads, chips)),
            dma((n_tp,)), dma((n_tp,)), dma((n_tp,)), dma((n_tp,)),
            dma((heads, n_tp)), dma((heads, n_tp)),
            dma((3, heads)),
        ],
        compiler_params=pltpu.CompilerParams(
            collective_id=0, has_side_effects=True, vmem_limit_bytes=63 * 2**20
        ),
        cost_estimate=pl.CostEstimate(
            flops=2 * rows * cols * n_tp * width + 12 * rows * BLOCK * width,
            bytes_accessed=2 * (out_weight.size + 4 * rows * width),
            transcendentals=3 * rows * BLOCK * heads,
        ),
    )(queries, key_rows, value_rows, selection.T, out_weight)


def solution(mesh):
    placed = (P("ctx", "tp"), P("ctx", "tp"), P("ctx", "tp"), P(), P("tp", None))
    body = functools.partial(per_device, mesh.shape["ctx"], mesh.shape["tp"])
    return jax.shard_map(
        body, mesh=mesh, in_specs=placed, out_specs=P("ctx", "tp"), check_vma=False
    )
```
